32 devices in a mesh: groups: 2 (over y), vocab: 16 (over z, x, core).
Axes of the slice: x: 2, y: 2, z: 4, core: 2. Of those that a mesh axis runs over, the one named last changes fastest.
Arguments:
- hidden: bfloat16 [128, 4096], P(('groups', 'vocab')), parts along dimension 0, may hold values from -2048 to 2048
- embedding: bfloat16 [16384, 4096], P(('groups', 'vocab')), parts along dimension 0, may hold values from -0.28125 to 0.28125
- d_input: bfloat16 [128, 4096], P(('groups', 'vocab')), parts along dimension 0, may hold values from -6 to 6
- input_ids: int32 [128], P('groups'), parts along dimension 0, may hold values from 0 to 8191
- language: int32 [128], P('groups'), parts along dimension 0, may hold values from 0 to 15
- allowed: int32 [32, 16], P('groups'), parts along dimension 0, may hold values from 0 to 1, as said below
- target: int32 [128], P('groups'), parts along dimension 0, may hold values from 0 to 8191, as said below
- token_weight: float32 [128], P('groups'), parts along dimension 0, may hold values from 4 to 32
Outputs:
- d_hidden: bfloat16 [128, 4096], P(('groups', 'vocab')), parts along dimension 0
- d_embed: bfloat16 [16384, 4096], P(('groups', 'vocab')), parts along dimension 0
The draws below stay inside these ranges and needn't reach their ends.
There are 2 independent parts, one for each index of `groups`. The reference program is written for one: setup_inputs(seed, part) draws one part's arguments, and reference() takes and returns one part's arrays. A program takes and returns all parts, laid end to end along the dimension named above; each array names one. Nothing has to cross between parts.
Inputs may be any that keep to these rules, and one draw needn't show every extreme that they name: `allowed`: every language allows at least one block. Each target lies in a block allowed for its token's language.
All inputs are finite; a program needn't handle non-finite values.
Results may differ from the reference program's by a relative error of at most 0.005.
Values may be sent and summed in bfloat16 or wider, within the bound.
No kernel may reach another device: no remote copies, remote signals or barrier semaphores. Data moves between devices by JAX's collectives and lax.ppermute only.
A program may use at most 128 MiB of HBM per device.

```python
import math
import jax
import jax.numpy as jnp
import numpy as np
from jax import lax

D = 4096
V_DEV = 512
NLANG = 16
TOKENS = 64
NBLK = 16
VOCAB = 8192


def token_tables(key):
    languages = jax.random.randint(jax.random.fold_in(key, 11), (TOKENS,), 0, NLANG)
    thresholds = jax.random.randint(jax.random.fold_in(key, 12), (NBLK,), 1, 10)
    chance_roll = jax.random.randint(jax.random.fold_in(key, 13), (NLANG, NBLK), 0, 10)
    forced = jax.random.randint(jax.random.fold_in(key, 14), (NLANG,), 0, NBLK)
    blocks = jnp.arange(NBLK, dtype=jnp.int32)
    allowed = ((chance_roll < thresholds[None, :]) | (blocks[None, :] == forced[:, None])).astype(jnp.int32)
    scores = allowed[languages] * 2 ** 20 + jax.random.randint(jax.random.fold_in(key, 15), (TOKENS, NBLK), 0, 2 ** 20)
    block_pick = jnp.argmax(scores, axis=1).astype(jnp.int32)
    offset = jax.random.randint(jax.random.fold_in(key, 16), (TOKENS,), 0, V_DEV - 1)
    targets = block_pick * V_DEV + offset
    return (languages.astype(jnp.int32), allowed, targets.astype(jnp.int32))


def table_row(key, index):
    row_key = jax.random.fold_in(jax.random.fold_in(key, 77), index)
    return jnp.clip(jax.random.normal(row_key, (D,), jnp.float32), -6.0, 6.0)


def draw_language(key, part):
    return token_tables(key)[0]


def draw_allowed(key, part):
    return token_tables(key)[1]


def draw_target(key, part):
    return token_tables(key)[2]


def draw_embedding(key, part):
    rows = jax.vmap(lambda index: table_row(key, index))(jnp.arange(VOCAB, dtype=jnp.int32))
    return (rows * (3.0 / 64.0)).astype(jnp.bfloat16)


def drawn_rows(key, targets, residue, base_level, level_step):
    positions = jnp.arange(TOKENS, dtype=jnp.int32)
    chosen = positions % 32 == residue
    level = base_level + level_step * (positions // 32 % 3).astype(jnp.float32)
    factor = level * (64.0 / (3.0 * D))
    first_rows = jax.vmap(lambda index: table_row(key, index))(targets)
    second_rows = jax.vmap(lambda index: table_row(key, index))(targets + 1)
    aligned = jnp.clip(factor[:, None] * (first_rows + second_rows) * 0.5, -2048.0, 2048.0)
    return (chosen, aligned)


def draw_hidden(key, part):
    targets = token_tables(key)[2]
    own_key = jax.random.fold_in(key, 3)
    draws = jnp.clip(jax.random.normal(own_key, (TOKENS, D), jnp.float32), -6.0, 6.0)
    chosen, aligned = drawn_rows(key, targets, 0, 110.0, 75.0)
    draws = jnp.where(chosen[:, None], aligned, draws)
    return draws.astype(jnp.bfloat16)


def touch_ends(entries, rng, low, largest):
    longest = entries.shape.index(max(entries.shape))
    spots = []
    for shift in (0, 1):
        where = [jax.random.randint(jax.random.fold_in(rng, axis), (), 0, length) for axis, length in enumerate(entries.shape)]
        where[longest] = (where[longest] + shift) % entries.shape[longest]
        spots.append(tuple(where))
    return entries.at[spots[0]].set(low).at[spots[1]].set(largest)


def block_scale(rng, dims, pieces, least, largest):
    gain = 1.0
    for position, blocks in pieces:
        heights = jax.random.uniform(jax.random.fold_in(jax.random.fold_in(rng, 6), position), (blocks,), jnp.float32, least / len(pieces), largest / len(pieces))
        gain = gain * jnp.repeat(jnp.exp(heights), dims[position] // blocks).reshape((-1,) + (1,) * (len(dims) - 1 - position))
    return gain


def rank_table(amount, lean):
    portions = [(1 << 20) // math.isqrt(grade ** lean) + 1 for grade in range(1, amount + 1)]
    deviation = 1 + sum(portions) // (1 << 30)
    return np.cumsum(np.array([max(1, weight // deviation) for weight in portions]))


def skewed_ids(key, shape, count, slope):
    table = rank_table(count, slope)
    ticket = jax.random.randint(jax.random.fold_in(key, 1), shape, 0, int(table[count - 1]))
    rank = jnp.searchsorted(jnp.asarray(table, jnp.int32), ticket, side="right")
    return jax.random.permutation(jax.random.fold_in(key, 2), count)[rank].astype(jnp.int32)


def gaussian(key, extent, deviation, bound, shards=(), held_as=jnp.bfloat16):
    array = deviation * jax.random.normal(key, extent, jnp.float32)
    if shards:
        array = array * block_scale(key, extent, shards, -0.22, 0.18)
    return jnp.clip(array, -bound, bound).astype(held_as)


def setup_inputs(seed: int = 0, part: int = 0) -> dict:
    key_of = jax.random.split(jax.random.key(seed), 9)
    part_splits = jax.random.split(jax.random.fold_in(key_of[8], part), 9)
    return {
        "hidden": draw_hidden(jax.random.fold_in(jax.random.fold_in(key_of[8], part), 71), part),
        "embedding": draw_embedding(jax.random.fold_in(jax.random.fold_in(key_of[8], part), 71), part),
        "d_input": gaussian(part_splits[2], (TOKENS, D), 1.0, 6.0, ((0, 16),)),
        "input_ids": touch_ends(skewed_ids(part_splits[3], (TOKENS,), VOCAB, 2), jax.random.fold_in(part_splits[3], 3), 0, VOCAB - 1).astype(jnp.int32),
        "language": draw_language(jax.random.fold_in(jax.random.fold_in(key_of[8], part), 71), part),
        "allowed": draw_allowed(jax.random.fold_in(jax.random.fold_in(key_of[8], part), 71), part),
        "target": draw_target(jax.random.fold_in(jax.random.fold_in(key_of[8], part), 71), part),
        "token_weight": jnp.clip(jnp.exp(jax.random.uniform(part_splits[7], (TOKENS,), jnp.float32, math.log(4.0), math.log(32.0))), 4.0, 32.0),
    }


def reference(hidden, embedding, d_input, input_ids, language, allowed, target, token_weight):
    logits = lax.dot_general(hidden, embedding, (((1,), (1,)), ((), ())), preferred_element_type=jnp.float32)
    allow_tok = allowed[language] > 0
    usable = jnp.repeat(allow_tok, V_DEV, axis=1)
    masked = jnp.where(usable, logits, jnp.float32(-1e+30))
    row_max = lax.optimization_barrier(jnp.max(masked, axis=1))
    shifted = jnp.exp(masked - row_max[:, None])
    row_total = lax.optimization_barrier(jnp.sum(jnp.where(usable, shifted, jnp.float32(0.0)), axis=1))
    columns = jnp.arange(VOCAB, dtype=jnp.int32)
    onehot = (columns[None, :] == target[:, None]).astype(jnp.float32)
    d_logits = jnp.where(usable, token_weight[:, None] * (shifted / row_total[:, None] - onehot), jnp.float32(0.0)).astype(jnp.bfloat16)
    d_hidden = jnp.dot(d_logits, embedding, preferred_element_type=jnp.float32).astype(jnp.bfloat16)
    grad_input = d_input.astype(jnp.float32)

    def block_grad(block):
        first = (block * V_DEV).astype(jnp.int32)
        part_logits = lax.dynamic_slice_in_dim(d_logits, first, V_DEV, 1)
        head = lax.dot_general(part_logits, hidden, (((0,), (0,)), ((), ())), preferred_element_type=jnp.float32)
        local_rows = input_ids - first
        valid = (local_rows >= 0) & (local_rows < V_DEV)
        local_rows = jnp.where(valid, local_rows, V_DEV).astype(jnp.int32)
        head = head.at[local_rows].add(grad_input, mode='drop')
        return head.astype(jnp.bfloat16)
    blocks = lax.map(block_grad, jnp.arange(NBLK, dtype=jnp.int32))
    return (d_hidden, blocks.reshape(VOCAB, D))
```

```python
import jax
import jax.numpy as jnp
from jax import lax
from jax.sharding import PartitionSpec as P

NEG = -1e30


def per_device(n, hidden, embedding, d_input, input_ids, language, allowed, target, token_weight):
    f32, bf16 = jnp.float32, jnp.bfloat16
    cols, width = embedding.shape
    mine = hidden.shape[0]
    tokens = mine * n
    steps = n.bit_length() - 1
    me = lax.axis_index("vocab")

    def swap(x, k):
        return lax.ppermute(x, "vocab", [(i, i ^ k) for i in range(n)])

    def bit(k):
        return (me & k) != 0

    def order(x):
        y = x.reshape((2,) * steps + (mine,) + x.shape[1:])
        perm = tuple(range(steps))[::-1] + tuple(range(steps, y.ndim))
        return y.transpose(perm).reshape(x.shape)

    def gather(x):
        k = n // 2
        while k:
            r = swap(x, k)
            x = jnp.where(bit(k), jnp.concatenate([r, x], 0), jnp.concatenate([x, r], 0))
            k //= 2
        return x

    def halves(x, k):
        h = x.shape[0] // 2
        a, b = x[:h], x[h:]
        return jnp.where(bit(k), b, a), jnp.where(bit(k), a, b)

    target, language, input_ids, weight = order(target), order(language), order(input_ids), order(token_weight)
    lang_allows = lax.dynamic_slice_in_dim(allowed, me, 1, 1)[:, 0]
    matches = language[:, None] == jnp.arange(allowed.shape[0], dtype=jnp.int32)[None, :]
    row_ok = jnp.sum(jnp.where(matches, lang_allows[None, :], 0), axis=1) > 0
    columns = me * cols + jnp.arange(cols, dtype=jnp.int32)
    is_target = columns[None, :] == target[:, None]

    rows = jnp.dot(is_target.astype(bf16), embedding, preferred_element_type=f32).astype(bf16)
    k = 1
    while k < n:
        keep, send = halves(rows, k)
        rows = keep + swap(send, k)
        k *= 2

    all_hidden = gather(hidden)
    all_input = gather(d_input)

    logits = lax.dot_general(all_hidden, embedding, (((1,), (1,)), ((), ())), preferred_element_type=f32)
    masked = jnp.where(row_ok[:, None], logits, f32(NEG))
    m = jnp.max(masked, axis=1)
    p = jnp.where(row_ok[:, None], jnp.exp(masked - m[:, None]), f32(0.0))
    s = jnp.sum(p, axis=1)
    lt = jnp.max(jnp.where(is_target, masked, f32(NEG)), axis=1)
    part = jnp.dot(jnp.where(is_target, f32(0.0), p).astype(bf16), embedding, preferred_element_type=f32)

    lo = 0
    k = 1
    while k < n:
        got = swap(jnp.stack([m, s, lt]), k)
        m_new = jnp.maximum(m, got[0])
        a, b = jnp.exp(m - m_new), jnp.exp(got[0] - m_new)
        s = s * a + got[1] * b
        lt = jnp.maximum(lt, got[2])
        keep, send = halves(part, k)
        recv = swap(send.astype(bf16), k).astype(f32)
        size = keep.shape[0]
        lo = lo + jnp.where(bit(k), size, 0)
        part = keep * lax.dynamic_slice_in_dim(a, lo, size)[:, None] + recv * lax.dynamic_slice_in_dim(b, lo, size)[:, None]
        m = m_new
        k *= 2

    d_logits = jnp.where(
        row_ok[:, None],
        weight[:, None] * (jnp.exp(masked - m[:, None]) / s[:, None] - is_target.astype(f32)),
        f32(0.0),
    ).astype(bf16)
    coef = (weight * (jnp.exp(lt - m) / s - 1.0)).astype(bf16).astype(f32)
    scale = weight / s
    d_hidden = (
        part * lax.dynamic_slice_in_dim(scale, lo, mine)[:, None]
        + rows.astype(f32) * lax.dynamic_slice_in_dim(coef, lo, mine)[:, None]
    ).astype(bf16)
    took = (columns[None, :] == input_ids[:, None]).astype(bf16)
    d_embed = lax.dot_general(
        jnp.concatenate([d_logits, took], 0),
        jnp.concatenate([all_hidden, all_input], 0),
        (((0,), (0,)), ((), ())),
        preferred_element_type=f32,
    ).astype(bf16)
    return d_hidden, d_embed


def solution(mesh):
    n = mesh.shape["vocab"]
    placed = (
        P(("groups", "vocab"), None),
        P(("groups", "vocab"), None),
        P(("groups", "vocab"), None),
        P("groups"),
        P("groups"),
        P("groups", None),
        P("groups"),
        P("groups"),
    )
    return jax.shard_map(
        lambda *args: per_device(n, *args),
        mesh=mesh,
        in_specs=placed,
        out_specs=(P(("groups", "vocab"), None), P(("groups", "vocab"), None)),
        check_vma=False,
    )
```

```python
import functools

import jax
import jax.numpy as jnp
from jax import lax
from jax.experimental import pallas as pl
from jax.experimental.pallas import tpu as pltpu
from jax.sharding import PartitionSpec as P

NEG = -1e30
f32, bf16, i32 = jnp.float32, jnp.bfloat16, jnp.int32


def prepare(mine, steps, me, hidden, d_input, ids, language, allowed, target, weight,
            hidden_o, input_o, pick_o, took_o, ok_o, weight_o):
    rank = me[0, 0]
    n = 1 << steps
    tokens = mine * n
    cols = pick_o.shape[1]
    hidden_o[...] = hidden[...]
    input_o[...] = d_input[...]
    place = lax.broadcasted_iota(i32, (tokens, 1), 0)
    block = lax.div(place, mine)
    source = place - block * mine
    for i in range(steps):
        source = source + mine * (n >> (i + 1)) * (lax.shift_right_logical(block, i) & 1)
    here = source == lax.broadcasted_iota(i32, (tokens, tokens), 1)

    def column(ref):
        return jnp.sum(jnp.where(here, ref[...], jnp.zeros_like(ref[...])), axis=1, keepdims=True)

    vocab = rank * cols + lax.broadcasted_iota(i32, (1, cols), 1)
    pick_o[...] = (column(target) == vocab).astype(f32).astype(bf16)
    took_o[...] = (column(ids) == vocab).astype(f32).astype(bf16)
    weight_o[...] = column(weight)
    langs, blocks = allowed.shape
    speaks = (column(language) == lax.broadcasted_iota(i32, (1, langs), 1)).astype(f32)
    may = jnp.dot(speaks, allowed[...].astype(f32), preferred_element_type=f32)
    column_here = lax.broadcasted_iota(i32, (1, blocks), 1) == rank
    ok_o[...] = jnp.sum(jnp.where(column_here, may, 0.0), axis=1, keepdims=True)


def per_device(n, hidden, embedding, d_input, input_ids, language, allowed, target, token_weight):
    cols, width = embedding.shape
    mine = hidden.shape[0]
    tokens = mine * n
    steps = n.bit_length() - 1
    me = lax.axis_index("vocab")

    def swap(x, k):
        return lax.ppermute(x, "vocab", [(i, i ^ k) for i in range(n)])

    def bit(k):
        return (me & k) != 0

    def after(x, *deps):
        return lax.optimization_barrier((x,) + deps)[0]

    def join(x, r, k):
        return jnp.where(bit(k), jnp.concatenate([r, x], 0), jnp.concatenate([x, r], 0))

    def halves(x, k):
        h = x.shape[0] // 2
        a, b = x[:h], x[h:]
        return jnp.where(bit(k), b, a), jnp.where(bit(k), a, b)

    first = swap(hidden, n // 2)
    first_input = swap(d_input, n // 2)
    vmem = pl.BlockSpec(memory_space=pltpu.VMEM)
    hidden_c, input_c, pick, took, ok, weight = pl.pallas_call(
        functools.partial(prepare, mine, steps),
        out_shape=(
            jax.ShapeDtypeStruct(hidden.shape, bf16),
            jax.ShapeDtypeStruct(d_input.shape, bf16),
            jax.ShapeDtypeStruct((tokens, cols), bf16),
            jax.ShapeDtypeStruct((tokens, cols), bf16),
            jax.ShapeDtypeStruct((tokens, 1), f32),
            jax.ShapeDtypeStruct((tokens, 1), f32),
        ),
        in_specs=[pl.BlockSpec(memory_space=pltpu.SMEM)] + [vmem] * 7,
        out_specs=(vmem,) * 6,
        name="prepare",
    )(
        me.reshape(1, 1), hidden, d_input, input_ids.reshape(1, tokens), language.reshape(1, tokens),
        allowed, target.reshape(1, tokens), token_weight.reshape(1, tokens),
    )
    usable = ok > 0.0
    is_target = pick > 0

    all_hidden, all_input = join(hidden_c, first, n // 2), join(input_c, first_input, n // 2)
    k = n // 4
    while k:
        if k == 2:
            all_input = after(all_input, all_hidden)
            pick_late = after(pick, all_hidden)
        got = swap(all_hidden, k)
        if k > 1:
            got_input = swap(all_input, k)
        all_hidden = join(all_hidden, got, k)
        if k > 2:
            all_input = join(all_input, got_input, k)
        k //= 2
    all_input = join(all_input, after(got_input, all_hidden), 2)
    all_input = join(all_input, swap(all_input, 1), 1)
    rows = jnp.dot(pick_late, embedding, preferred_element_type=f32).astype(bf16)
    keep, send = halves(rows, 1)
    rows = keep + swap(send, 1)

    logits = lax.dot_general(all_hidden, embedding, (((1,), (1,)), ((), ())), preferred_element_type=f32)
    masked = jnp.where(usable, logits, f32(NEG))
    m = jnp.max(masked, axis=1)
    p = jnp.where(usable, jnp.exp(masked - m[:, None]), f32(0.0))
    s = jnp.sum(p, axis=1)
    lt = jnp.max(jnp.where(is_target, masked, f32(NEG)), axis=1)
    part = jnp.dot(jnp.where(is_target, f32(0.0), p).astype(bf16), embedding, preferred_element_type=f32)

    lo = 0
    k = 1
    while k < n:
        keep, send = halves(part, k)
        send = send.astype(bf16)
        packed = jnp.stack([m, s, lt])
        if k > 1:
            packed, send = lax.optimization_barrier((packed, send))
            keep_rows, send_rows = halves(after(rows, packed), k)
        got = swap(packed, k)
        recv = swap(send, k)
        if k > 1:
            rows = keep_rows + swap(send_rows, k)
        m_new = jnp.maximum(m, got[0])
        a, b = jnp.exp(m - m_new), jnp.exp(got[0] - m_new)
        s = s * a + got[1] * b
        lt = jnp.maximum(lt, got[2])
        m, s, lt, a, b = lax.optimization_barrier((m_new, s, lt, a, b))
        size = keep.shape[0]
        lo = lo + jnp.where(bit(k), size, 0)
        part = keep * lax.dynamic_slice_in_dim(a, lo, size)[:, None] + recv.astype(f32) * lax.dynamic_slice_in_dim(b, lo, size)[:, None]
        k *= 2

    hot = is_target.astype(f32)
    d_logits = jnp.where(
        usable, weight * (jnp.exp(masked - m[:, None]) / s[:, None] - hot), f32(0.0)
    ).astype(bf16)
    w = weight[:, 0]
    coef = (w * (jnp.exp(lt - m) / s - 1.0)).astype(bf16).astype(f32)
    scale = w / s
    d_hidden = (
        part * lax.dynamic_slice_in_dim(scale, lo, mine)[:, None]
        + rows.astype(f32) * lax.dynamic_slice_in_dim(coef, lo, mine)[:, None]
    ).astype(bf16)
    d_embed = lax.dot_general(
        jnp.concatenate([d_logits, took], 0),
        jnp.concatenate([all_hidden, all_input], 0),
        (((0,), (0,)), ((), ())),
        preferred_element_type=f32,
    ).astype(bf16)
    return d_hidden, d_embed


def solution(mesh):
    n = mesh.shape["vocab"]
    placed = (
        P(("groups", "vocab"), None),
        P(("groups", "vocab"), None),
        P(("groups", "vocab"), None),
        P("groups"),
        P("groups"),
        P("groups", None),
        P("groups"),
        P("groups"),
    )
    return jax.shard_map(
        functools.partial(per_device, n),
        mesh=mesh,
        in_specs=placed,
        out_specs=(P(("groups", "vocab"), None), P(("groups", "vocab"), None)),
        check_vma=False,
    )
```

```python
import functools

import jax
import jax.numpy as jnp
from jax import lax
from jax.experimental import pallas as pl
from jax.experimental.pallas import tpu as pltpu
from jax.sharding import PartitionSpec as P

NEG = -1e30
f32, bf16, i32 = jnp.float32, jnp.bfloat16, jnp.int32


def prepare(mine, steps, me, table_h, ids_h, language_h, allowed_h, target_h, weight_h,
            code_o, took_o, weight_o, pick_o,
            ids, language, allowed, target, weight, sem):
    del table_h
    small = [
        pltpu.make_async_copy(src, dst, sem.at[i])
        for i, (src, dst) in enumerate((
            (target_h, target), (ids_h, ids), (language_h, language), (weight_h, weight), (allowed_h, allowed)))
    ]
    for copy in small:
        copy.start()
    for copy in small:
        copy.wait()
    rank = me[0, 0]
    n = 1 << steps
    tokens = mine * n
    half = tokens // 2
    cols = took_o.shape[1]
    place = lax.broadcasted_iota(i32, (tokens, 1), 0)
    block = lax.div(place, mine)
    source = place - block * mine
    for i in range(steps):
        source = source + mine * (n >> (i + 1)) * (lax.shift_right_logical(block, i) & 1)
    here = source == lax.broadcasted_iota(i32, (tokens, tokens), 1)

    def column(ref):
        return jnp.sum(jnp.where(here, ref[...], jnp.zeros_like(ref[...])), axis=1, keepdims=True)

    vocab = rank * cols + lax.broadcasted_iota(i32, (1, cols), 1)
    pick = (column(target) == vocab).astype(f32)
    took_o[...] = (column(ids) == vocab).astype(f32).astype(bf16)
    langs, blocks = allowed.shape
    speaks = (column(language) == lax.broadcasted_iota(i32, (1, langs), 1)).astype(f32)
    may = jnp.dot(speaks, allowed[...].astype(f32), preferred_element_type=f32)
    column_here = lax.broadcasted_iota(i32, (1, blocks), 1) == rank
    ok = jnp.sum(jnp.where(column_here, may, 0.0), axis=1, keepdims=True)
    code_o[...] = (jnp.where(ok > 0.0, 1.0, 0.0) * (1.0 + pick)).astype(bf16)
    weight_o[...] = jnp.broadcast_to(column(weight), weight_o.shape)
    upper = (rank & 1) == 1
    pick_o[...] = jnp.where(upper, jnp.concatenate([pick[half:], pick[:half]], 0), pick).astype(bf16)


def per_device(n, hidden, embedding, d_input, input_ids, language, allowed, target, token_weight):
    cols, width = embedding.shape
    mine = hidden.shape[0]
    tokens = mine * n
    steps = n.bit_length() - 1
    me = lax.axis_index("vocab")

    def swap(x, k):
        return lax.ppermute(x, "vocab", [(i, i ^ k) for i in range(n)])

    def bit(k):
        return (me & k) != 0

    def after(x, *deps):
        return lax.optimization_barrier((x,) + deps)[0]

    def join(x, r, k):
        return jnp.where(bit(k), jnp.concatenate([r, x], 0), jnp.concatenate([x, r], 0))

    def halves(x, k):
        h = x.shape[0] // 2
        a, b = x[:h], x[h:]
        return jnp.where(bit(k), b, a), jnp.where(bit(k), a, b)

    first = swap(hidden, n // 2)
    first_input = swap(d_input, n // 2)
    vmem, hbm = pl.BlockSpec(memory_space=pltpu.VMEM), pl.BlockSpec(memory_space=pltpu.HBM)
    code, took, weight, pick = pl.pallas_call(
        functools.partial(prepare, mine, steps),
        out_shape=(
            jax.ShapeDtypeStruct((tokens, cols), bf16),
            jax.ShapeDtypeStruct((tokens, cols), bf16),
            jax.ShapeDtypeStruct((tokens, cols), f32),
            jax.ShapeDtypeStruct((tokens, cols), bf16),
        ),
        in_specs=[pl.BlockSpec(memory_space=pltpu.SMEM)] + [hbm] * 6,
        out_specs=(vmem,) * 4,
        scratch_shapes=[
            pltpu.VMEM((1, tokens), i32),
            pltpu.VMEM((1, tokens), i32),
            pltpu.VMEM(allowed.shape, i32),
            pltpu.VMEM((1, tokens), i32),
            pltpu.VMEM((1, tokens), f32),
            pltpu.SemaphoreType.DMA((5,)),
        ],
        compiler_params=pltpu.CompilerParams(vmem_limit_bytes=60 * 1024 * 1024),
        name="prepare",
    )(
        me.reshape(1, 1), embedding, input_ids.reshape(1, tokens), language.reshape(1, tokens),
        allowed, target.reshape(1, tokens), token_weight.reshape(1, tokens),
    )
    usable = code > 0
    is_target = code > 1

    k = n // 2
    all_hidden, all_input = join(hidden, first, k), join(d_input, first_input, k)
    k //= 2
    while k > 2:
        got, got_input = swap(all_hidden, k), swap(all_input, k)
        all_hidden, all_input = join(all_hidden, got, k), join(all_input, got_input, k)
        k //= 2
    got = swap(all_hidden, 2)
    half = tokens // 2
    rows = jnp.dot(after(pick, all_hidden), embedding, preferred_element_type=f32).astype(bf16)
    rows = rows[:half] + swap(rows[half:], 1)
    rows_keep, rows_send = halves(rows, 2)
    rows_got = swap(rows_send, 2)
    input_got = swap(after(all_input, all_hidden), 2)
    all_hidden = join(all_hidden, got, 2)
    all_hidden = join(all_hidden, swap(all_hidden, 1), 1)

    logits = lax.dot_general(all_hidden, embedding, (((1,), (1,)), ((), ())), preferred_element_type=f32)
    masked = jnp.where(usable, logits, f32(NEG))
    m = jnp.max(masked, axis=1)
    p = jnp.where(usable, jnp.exp(masked - m[:, None]), f32(0.0))
    s = jnp.sum(p, axis=1)
    lt = jnp.max(jnp.where(is_target, masked, f32(NEG)), axis=1)
    p = after(jnp.where(is_target, f32(0.0), p).astype(bf16), m, s, lt)
    part = jnp.dot(p, embedding, preferred_element_type=f32)

    lo = 0
    k = 1
    while k < n:
        last = k == n // 2
        keep, send = halves(part, k)
        send = send.astype(bf16)
        if last:
            rows_keep, rows_send = halves(rows, k)
            send = jnp.concatenate([send, rows_send], 0)
        packed = jnp.stack([m, s, lt])
        if k > 1:
            packed, send = lax.optimization_barrier((packed, send))
        got = swap(packed, k)
        recv = swap(send, k)
        size = keep.shape[0]
        if last:
            rows = rows_keep + recv[size:]
        m_new = jnp.maximum(m, got[0])
        a, b = jnp.exp(m - m_new), jnp.exp(got[0] - m_new)
        s = s * a + got[1] * b
        lt = jnp.maximum(lt, got[2])
        m, s, lt, a, b = lax.optimization_barrier((m_new, s, lt, a, b))
        if k == 1:
            rows = rows_keep + after(rows_got, m)
            all_input = join(all_input, after(input_got, m), 2)
            all_input = join(all_input, swap(all_input, 1), 1)
        elif 2 < k < n // 2:
            rows = rows_keep + after(rows_got, m)
        if 1 < k < n // 4:
            rows_keep, rows_send = halves(after(rows, m), 2 * k)
            rows_got = swap(rows_send, 2 * k)
        lo = lo + jnp.where(bit(k), size, 0)
        part = keep * lax.dynamic_slice_in_dim(a, lo, size)[:, None] + recv[:size].astype(f32) * lax.dynamic_slice_in_dim(b, lo, size)[:, None]
        k *= 2

    hot = is_target.astype(f32)
    d_logits = jnp.where(
        usable, weight * (jnp.exp(masked - m[:, None]) / s[:, None] - hot), f32(0.0)
    ).astype(bf16)
    w = lax.dynamic_slice_in_dim(token_weight, me * mine, mine)
    m_own, s_own, lt_own = (lax.dynamic_slice_in_dim(x, lo, mine) for x in (m, s, lt))
    coef = (w * (jnp.exp(lt_own - m_own) / s_own - 1.0)).astype(bf16).astype(f32)
    d_hidden = (part * (w / s_own)[:, None] + rows.astype(f32) * coef[:, None]).astype(bf16)
    d_embed = lax.dot_general(
        jnp.concatenate([d_logits, took], 0),
        jnp.concatenate([all_hidden, all_input], 0),
        (((0,), (0,)), ((), ())),
        preferred_element_type=f32,
    ).astype(bf16)
    return d_hidden, d_embed


def solution(mesh):
    n = mesh.shape["vocab"]
    placed = (
        P(("groups", "vocab"), None),
        P(("groups", "vocab"), None),
        P(("groups", "vocab"), None),
        P("groups"),
        P("groups"),
        P("groups", None),
        P("groups"),
        P("groups"),
    )
    return jax.shard_map(
        functools.partial(per_device, n),
        mesh=mesh,
        in_specs=placed,
        out_specs=(P(("groups", "vocab"), None), P(("groups", "vocab"), None)),
        check_vma=False,
    )
```

```python
import functools

import jax
import jax.numpy as jnp
from jax import lax
from jax.experimental import pallas as pl
from jax.experimental.pallas import tpu as pltpu
from jax.sharding import PartitionSpec as P

NEG = -1e30
f32, bf16, i32 = jnp.float32, jnp.bfloat16, jnp.int32


def prepare(mine, steps, me, table_h, ids_h, language_h, allowed_h, target_h, weight_h,
            code_o, took_o, weight_o, pick_o,
            ids, language, allowed, target, weight, sem):
    del table_h
    small = [
        pltpu.make_async_copy(src, dst, sem.at[i])
        for i, (src, dst) in enumerate((
            (target_h, target), (ids_h, ids), (language_h, language), (weight_h, weight), (allowed_h, allowed)))
    ]
    for copy in small:
        copy.start()
    for copy in small:
        copy.wait()
    rank = me[0, 0]
    n = 1 << steps
    tokens = mine * n
    half = tokens // 2
    cols = took_o.shape[1]
    place = lax.broadcasted_iota(i32, (tokens, 1), 0)
    block = lax.div(place, mine)
    source = place - block * mine
    for i in range(steps):
        source = source + mine * (n >> (i + 1)) * (lax.shift_right_logical(block, i) & 1)
    here = source == lax.broadcasted_iota(i32, (tokens, tokens), 1)

    def column(ref):
        return jnp.sum(jnp.where(here, ref[...], jnp.zeros_like(ref[...])), axis=1, keepdims=True)

    vocab = rank * cols + lax.broadcasted_iota(i32, (1, cols), 1)
    pick = (column(target) == vocab).astype(f32)
    took_o[...] = (column(ids) == vocab).astype(f32).astype(bf16)
    langs, blocks = allowed.shape
    speaks = (column(language) == lax.broadcasted_iota(i32, (1, langs), 1)).astype(f32)
    may = jnp.dot(speaks, allowed[...].astype(f32), preferred_element_type=f32)
    column_here = lax.broadcasted_iota(i32, (1, blocks), 1) == rank
    ok = jnp.sum(jnp.where(column_here, may, 0.0), axis=1, keepdims=True)
    code_o[...] = (jnp.where(ok > 0.0, 1.0, 0.0) * (1.0 + pick)).astype(bf16)
    weight_o[...] = jnp.broadcast_to(column(weight), weight_o.shape)
    upper = (rank & 1) == 1
    pick_o[...] = jnp.where(upper, jnp.concatenate([pick[half:], pick[:half]], 0), pick).astype(bf16)


def table_grad(tiles, dl, took, hid, inp, out, held, sem):
    lhs = jnp.concatenate([dl[...], took[...]], 0).T
    step = out.shape[1] // tiles
    leaving = []
    for i in range(tiles):
        at = pl.ds(i * step, step)
        rhs = jnp.concatenate([hid[:, at], inp[:, at]], 0)
        held[:, at] = jnp.dot(lhs, rhs, preferred_element_type=f32).astype(bf16)
        leaving.append(pltpu.make_async_copy(held.at[:, at], out.at[:, at], sem.at[i]))
        leaving[-1].start()
    for copy in leaving:
        copy.wait()


def per_device(n, hidden, embedding, d_input, input_ids, language, allowed, target, token_weight):
    cols, width = embedding.shape
    mine = hidden.shape[0]
    tokens = mine * n
    steps = n.bit_length() - 1
    me = lax.axis_index("vocab")

    def swap(x, k):
        return lax.ppermute(x, "vocab", [(i, i ^ k) for i in range(n)])

    def bit(k):
        return (me & k) != 0

    def after(x, *deps):
        return lax.optimization_barrier((x,) + deps)[0]

    def join(x, r, k):
        return jnp.where(bit(k), jnp.concatenate([r, x], 0), jnp.concatenate([x, r], 0))

    def halves(x, k):
        h = x.shape[0] // 2
        a, b = x[:h], x[h:]
        return jnp.where(bit(k), b, a), jnp.where(bit(k), a, b)

    first = swap(hidden, n // 2)
    first_input = swap(d_input, n // 2)
    vmem, hbm = pl.BlockSpec(memory_space=pltpu.VMEM), pl.BlockSpec(memory_space=pltpu.HBM)
    code, took, weight, pick = pl.pallas_call(
        functools.partial(prepare, mine, steps),
        out_shape=(
            jax.ShapeDtypeStruct((tokens, cols), bf16),
            jax.ShapeDtypeStruct((tokens, cols), bf16),
            jax.ShapeDtypeStruct((tokens, cols), f32),
            jax.ShapeDtypeStruct((tokens, cols), bf16),
        ),
        in_specs=[pl.BlockSpec(memory_space=pltpu.SMEM)] + [hbm] * 6,
        out_specs=(vmem,) * 4,
        scratch_shapes=[
            pltpu.VMEM((1, tokens), i32),
            pltpu.VMEM((1, tokens), i32),
            pltpu.VMEM(allowed.shape, i32),
            pltpu.VMEM((1, tokens), i32),
            pltpu.VMEM((1, tokens), f32),
            pltpu.SemaphoreType.DMA((5,)),
        ],
        compiler_params=pltpu.CompilerParams(vmem_limit_bytes=60 * 1024 * 1024),
        name="prepare",
    )(
        me.reshape(1, 1), embedding, input_ids.reshape(1, tokens), language.reshape(1, tokens),
        allowed, target.reshape(1, tokens), token_weight.reshape(1, tokens),
    )
    usable = code > 0
    is_target = code > 1

    k = n // 2
    all_hidden, all_input = join(hidden, first, k), join(d_input, first_input, k)
    k //= 2
    while k > 2:
        got, got_input = swap(all_hidden, k), swap(all_input, k)
        all_hidden, all_input = join(all_hidden, got, k), join(all_input, got_input, k)
        k //= 2
    got = swap(all_hidden, 2)
    half = tokens // 2
    rows = jnp.dot(after(pick, all_hidden), embedding, preferred_element_type=f32).astype(bf16)
    rows = rows[:half] + swap(rows[half:], 1)
    rows_keep, rows_send = halves(rows, 2)
    rows_got = swap(rows_send, 2)
    all_hidden = join(all_hidden, got, 2)
    input_got = swap(after(all_input, all_hidden), 2)
    all_hidden = join(all_hidden, swap(all_hidden, 1), 1)

    logits = lax.dot_general(all_hidden, embedding, (((1,), (1,)), ((), ())), preferred_element_type=f32)
    masked = jnp.where(usable, logits, f32(NEG))
    m = jnp.max(masked, axis=1)
    p = jnp.where(usable, jnp.exp(masked - m[:, None]), f32(0.0))
    s = jnp.sum(p, axis=1)
    lt = jnp.max(jnp.where(is_target, masked, f32(NEG)), axis=1)
    p = after(jnp.where(is_target, f32(0.0), p).astype(bf16), m, s, lt)
    part = jnp.dot(p, embedding, preferred_element_type=f32)

    lo = 0
    k = 1
    while k < n:
        last = k == n // 2
        keep, send = halves(part, k)
        send = send.astype(bf16)
        if last:
            rows_keep, rows_send = halves(rows, k)
            send = jnp.concatenate([send, rows_send], 0)
        packed = jnp.stack([m, s, lt])
        if k > 1:
            packed, send = lax.optimization_barrier((packed, send))
        got = swap(packed, k)
        recv = swap(send, k)
        size = keep.shape[0]
        if last:
            rows = rows_keep + recv[size:]
        m_new = jnp.maximum(m, got[0])
        a, b = jnp.exp(m - m_new), jnp.exp(got[0] - m_new)
        s = s * a + got[1] * b
        lt = jnp.maximum(lt, got[2])
        m, s, lt, a, b = lax.optimization_barrier((m_new, s, lt, a, b))
        if k == 1:
            all_input = join(all_input, after(input_got, m), 2)
            all_input = join(all_input, swap(all_input, 1), 1)
        elif 2 < k < n // 2:
            rows = rows_keep + after(rows_got, m)
        if 1 < k < n // 4:
            rows_keep, rows_send = halves(after(rows, m), 2 * k)
            rows_got = swap(rows_send, 2 * k)
        lo = lo + jnp.where(bit(k), size, 0)
        part = keep * lax.dynamic_slice_in_dim(a, lo, size)[:, None] + recv[:size].astype(f32) * lax.dynamic_slice_in_dim(b, lo, size)[:, None]
        if k == 1:
            rows = rows_keep + after(rows_got, part)
        k *= 2

    hot = is_target.astype(f32)
    d_logits = jnp.where(
        usable, weight * (jnp.exp(masked - m[:, None]) / s[:, None] - hot), f32(0.0)
    ).astype(bf16)
    w = lax.dynamic_slice_in_dim(token_weight, me * mine, mine)
    m_own, s_own, lt_own = (lax.dynamic_slice_in_dim(x, lo, mine) for x in (m, s, lt))
    coef = (w * (jnp.exp(lt_own - m_own) / s_own - 1.0)).astype(bf16).astype(f32)
    d_hidden = (part * (w / s_own)[:, None] + rows.astype(f32) * coef[:, None]).astype(bf16)
    tiles = 8
    d_embed = pl.pallas_call(
        functools.partial(table_grad, tiles),
        out_shape=jax.ShapeDtypeStruct((cols, width), bf16),
        in_specs=[vmem] * 4,
        out_specs=hbm,
        scratch_shapes=[pltpu.VMEM((cols, width), bf16), pltpu.SemaphoreType.DMA((tiles,))],
        compiler_params=pltpu.CompilerParams(vmem_limit_bytes=24 * 1024 * 1024),
        cost_estimate=pl.CostEstimate(
            flops=4 * tokens * cols * width, bytes_accessed=2 * cols * width, transcendentals=0),
        name="table_grad",
    )(d_logits, took, all_hidden, all_input)
    return d_hidden, d_embed


def solution(mesh):
    n = mesh.shape["vocab"]
    placed = (
        P(("groups", "vocab"), None),
        P(("groups", "vocab"), None),
        P(("groups", "vocab"), None),
        P("groups"),
        P("groups"),
        P("groups", None),
        P("groups"),
        P("groups"),
    )
    return jax.shard_map(
        functools.partial(per_device, n),
        mesh=mesh,
        in_specs=placed,
        out_specs=(P(("groups", "vocab"), None), P(("groups", "vocab"), None)),
        check_vma=False,
    )
```

```python
import functools

import jax
import jax.numpy as jnp
from jax import lax
from jax.experimental import pallas as pl
from jax.experimental.pallas import tpu as pltpu
from jax.sharding import PartitionSpec as P

NEG = -1e30
f32, bf16, i32 = jnp.float32, jnp.bfloat16, jnp.int32


def partners(n, k):
    return {2: (2, 4), 4: (4, 8), 8: (8, 2)}.get(k, (k, k)) if n >= 16 else (k, k)


def prepare(mine, steps, me, table_h, ids_h, language_h, allowed_h, target_h, weight_h,
            code_o, took_o, weight_o, pick_o,
            ids, language, allowed, target, weight, sem):
    del table_h
    small = [
        pltpu.make_async_copy(src, dst, sem.at[i])
        for i, (src, dst) in enumerate((
            (target_h, target), (ids_h, ids), (language_h, language), (weight_h, weight), (allowed_h, allowed)))
    ]
    for copy in small:
        copy.start()
    for copy in small:
        copy.wait()
    rank = me[0, 0]
    n = 1 << steps
    tokens = mine * n
    half = tokens // 2
    cols = took_o.shape[1]
    place = lax.broadcasted_iota(i32, (tokens, 1), 0)
    block = lax.div(place, mine)
    source = place - block * mine
    odd = lax.shift_right_logical(block, steps - 1) & 1
    for i in range(steps):
        even_k, odd_k = partners(n, n >> (i + 1))
        source = source + mine * jnp.where(odd == 1, odd_k, even_k) * (lax.shift_right_logical(block, i) & 1)
    here = source == lax.broadcasted_iota(i32, (tokens, tokens), 1)

    def column(ref):
        return jnp.sum(jnp.where(here, ref[...], jnp.zeros_like(ref[...])), axis=1, keepdims=True)

    vocab = rank * cols + lax.broadcasted_iota(i32, (1, cols), 1)
    pick = (column(target) == vocab).astype(f32)
    took_o[...] = (column(ids) == vocab).astype(f32).astype(bf16)
    langs, blocks = allowed.shape
    speaks = (column(language) == lax.broadcasted_iota(i32, (1, langs), 1)).astype(f32)
    may = jnp.dot(speaks, allowed[...].astype(f32), preferred_element_type=f32)
    column_here = lax.broadcasted_iota(i32, (1, blocks), 1) == rank
    ok = jnp.sum(jnp.where(column_here, may, 0.0), axis=1, keepdims=True)
    code_o[...] = (jnp.where(ok > 0.0, 1.0, 0.0) * (1.0 + pick)).astype(bf16)
    weight_o[...] = jnp.broadcast_to(column(weight), weight_o.shape)
    upper = (rank & 1) == 1
    pick_o[...] = jnp.where(upper, jnp.concatenate([pick[half:], pick[:half]], 0), pick).astype(bf16)


def table_grad(tiles, dl, took, hid, inp, out, held, sem):
    lhs = jnp.concatenate([dl[...], took[...]], 0).T
    step = out.shape[1] // tiles
    leaving = []
    for i in range(tiles):
        at = pl.ds(i * step, step)
        rhs = jnp.concatenate([hid[:, at], inp[:, at]], 0)
        held[:, at] = jnp.dot(lhs, rhs, preferred_element_type=f32).astype(bf16)
        leaving.append(pltpu.make_async_copy(held.at[:, at], out.at[:, at], sem.at[i]))
        leaving[-1].start()
    for copy in leaving:
        copy.wait()


def per_device(n, hidden, embedding, d_input, input_ids, language, allowed, target, token_weight):
    cols, width = embedding.shape
    mine = hidden.shape[0]
    tokens = mine * n
    steps = n.bit_length() - 1
    me = lax.axis_index("vocab")

    def swap(x, k):
        ks = partners(n, k)
        return lax.ppermute(x, "vocab", [(i, i ^ ks[i & 1]) for i in range(n)])

    def bit(k):
        even_k, odd_k = partners(n, k)
        return (me & jnp.where((me & 1) == 1, odd_k, even_k)) != 0

    def after(x, *deps):
        return lax.optimization_barrier((x,) + deps)[0]

    def join(x, r, k):
        return jnp.where(bit(k), jnp.concatenate([r, x], 0), jnp.concatenate([x, r], 0))

    def halves(x, k):
        h = x.shape[0] // 2
        a, b = x[:h], x[h:]
        return jnp.where(bit(k), b, a), jnp.where(bit(k), a, b)

    first = swap(hidden, n // 2)
    first_input = swap(d_input, n // 2)
    vmem, hbm = pl.BlockSpec(memory_space=pltpu.VMEM), pl.BlockSpec(memory_space=pltpu.HBM)
    code, took, weight, pick = pl.pallas_call(
        functools.partial(prepare, mine, steps),
        out_shape=(
            jax.ShapeDtypeStruct((tokens, cols), bf16),
            jax.ShapeDtypeStruct((tokens, cols), bf16),
            jax.ShapeDtypeStruct((tokens, cols), f32),
            jax.ShapeDtypeStruct((tokens, cols), bf16),
        ),
        in_specs=[pl.BlockSpec(memory_space=pltpu.SMEM)] + [hbm] * 6,
        out_specs=(vmem,) * 4,
        scratch_shapes=[
            pltpu.VMEM((1, tokens), i32),
            pltpu.VMEM((1, tokens), i32),
            pltpu.VMEM(allowed.shape, i32),
            pltpu.VMEM((1, tokens), i32),
            pltpu.VMEM((1, tokens), f32),
            pltpu.SemaphoreType.DMA((5,)),
        ],
        compiler_params=pltpu.CompilerParams(vmem_limit_bytes=60 * 1024 * 1024),
        name="prepare",
    )(
        me.reshape(1, 1), embedding, input_ids.reshape(1, tokens), language.reshape(1, tokens),
        allowed, target.reshape(1, tokens), token_weight.reshape(1, tokens),
    )
    usable = code > 0
    is_target = code > 1

    k = n // 2
    all_hidden, all_input = join(hidden, first, k), join(d_input, first_input, k)
    k //= 2
    while k > 2:
        got, got_input = swap(all_hidden, k), swap(all_input, k)
        all_hidden, all_input = join(all_hidden, got, k), join(all_input, got_input, k)
        k //= 2
    got = swap(all_hidden, 2)
    half = tokens // 2
    rows = jnp.dot(after(pick, all_hidden), embedding, preferred_element_type=f32).astype(bf16)
    rows = rows[:half] + swap(rows[half:], 1)
    rows_keep, rows_send = halves(rows, 2)
    rows_got = swap(rows_send, 2)
    all_hidden = join(all_hidden, got, 2)
    input_got = swap(after(all_input, all_hidden), 2)
    all_hidden = join(all_hidden, swap(all_hidden, 1), 1)

    logits = lax.dot_general(all_hidden, embedding, (((1,), (1,)), ((), ())), preferred_element_type=f32)
    masked = jnp.where(usable, logits, f32(NEG))
    m = jnp.max(masked, axis=1)
    p = jnp.where(usable, jnp.exp(masked - m[:, None]), f32(0.0))
    s = jnp.sum(p, axis=1)
    lt = jnp.max(jnp.where(is_target, masked, f32(NEG)), axis=1)
    p = after(jnp.where(is_target, f32(0.0), p).astype(bf16), m, s, lt)
    part = jnp.dot(p, embedding, preferred_element_type=f32)

    lo = 0
    k = 1
    while k < n:
        last = k == n // 2
        keep, send = halves(part, k)
        send = send.astype(bf16)
        if last:
            rows_keep, rows_send = halves(rows, k)
            send = jnp.concatenate([send, rows_send], 0)
        packed = jnp.stack([m, s, lt])
        if k > 1:
            packed, send = lax.optimization_barrier((packed, send))
        got = swap(packed, k)
        recv = swap(send, k)
        size = keep.shape[0]
        if last:
            rows = rows_keep + recv[size:]
        m_new = jnp.maximum(m, got[0])
        a, b = jnp.exp(m - m_new), jnp.exp(got[0] - m_new)
        s = s * a + got[1] * b
        lt = jnp.maximum(lt, got[2])
        m, s, lt, a, b = lax.optimization_barrier((m_new, s, lt, a, b))
        if k == 1:
            all_input = join(all_input, after(input_got, m), 2)
            all_input = join(all_input, swap(all_input, 1), 1)
        elif 2 < k < n // 2:
            rows = rows_keep + after(rows_got, m)
        if 1 < k < n // 4:
            rows_keep, rows_send = halves(after(rows, m), 2 * k)
            rows_got = swap(rows_send, 2 * k)
        lo = lo + jnp.where(bit(k), size, 0)
        part = keep * lax.dynamic_slice_in_dim(a, lo, size)[:, None] + recv[:size].astype(f32) * lax.dynamic_slice_in_dim(b, lo, size)[:, None]
        if k == 1:
            rows = rows_keep + after(rows_got, part)
        k *= 2

    hot = is_target.astype(f32)
    d_logits = jnp.where(
        usable, weight * (jnp.exp(masked - m[:, None]) / s[:, None] - hot), f32(0.0)
    ).astype(bf16)
    w = lax.dynamic_slice_in_dim(token_weight, me * mine, mine)
    m_own, s_own, lt_own = (lax.dynamic_slice_in_dim(x, lo, mine) for x in (m, s, lt))
    coef = (w * (jnp.exp(lt_own - m_own) / s_own - 1.0)).astype(bf16).astype(f32)
    d_hidden = (part * (w / s_own)[:, None] + rows.astype(f32) * coef[:, None]).astype(bf16)
    tiles = 8
    d_embed = pl.pallas_call(
        functools.partial(table_grad, tiles),
        out_shape=jax.ShapeDtypeStruct((cols, width), bf16),
        in_specs=[vmem] * 4,
        out_specs=hbm,
        scratch_shapes=[pltpu.VMEM((cols, width), bf16), pltpu.SemaphoreType.DMA((tiles,))],
        compiler_params=pltpu.CompilerParams(vmem_limit_bytes=24 * 1024 * 1024),
        cost_estimate=pl.CostEstimate(
            flops=4 * tokens * cols * width, bytes_accessed=2 * cols * width, transcendentals=0),
        name="table_grad",
    )(d_logits, took, all_hidden, all_input)
    return d_hidden, d_embed


def solution(mesh):
    n = mesh.shape["vocab"]
    placed = (
        P(("groups", "vocab"), None),
        P(("groups", "vocab"), None),
        P(("groups", "vocab"), None),
        P("groups"),
        P("groups"),
        P("groups", None),
        P("groups"),
        P("groups"),
    )
    return jax.shard_map(
        functools.partial(per_device, n),
        mesh=mesh,
        in_specs=placed,
        out_specs=(P(("groups", "vocab"), None), P(("groups", "vocab"), None)),
        check_vma=False,
    )
```

```python
import functools

import jax
import jax.numpy as jnp
from jax import lax
from jax.experimental import pallas as pl
from jax.experimental.pallas import tpu as pltpu
from jax.sharding import PartitionSpec as P

NEG = -1e30
f32, bf16, i32 = jnp.float32, jnp.bfloat16, jnp.int32


def partners(n, k):
    return {2: (2, 4), 4: (4, 8), 8: (8, 2)}.get(k, (k, k)) if n >= 16 else (k, k)


def prepare(mine, steps, me, table_h, ids_h, language_h, allowed_h, target_h, weight_h,
            code_o, took_o, weight_o, pick_o,
            ids, language, allowed, target, weight, sem):
    del table_h
    small = [
        pltpu.make_async_copy(src, dst, sem.at[i])
        for i, (src, dst) in enumerate((
            (target_h, target), (ids_h, ids), (language_h, language), (weight_h, weight), (allowed_h, allowed)))
    ]
    for copy in small:
        copy.start()
    for copy in small:
        copy.wait()
    rank = me[0, 0]
    n = 1 << steps
    tokens = mine * n
    half = tokens // 2
    cols = took_o.shape[1]
    place = lax.broadcasted_iota(i32, (tokens, 1), 0)
    block = lax.div(place, mine)
    source = place - block * mine
    odd = lax.shift_right_logical(block, steps - 1) & 1
    for i in range(steps):
        even_k, odd_k = partners(n, n >> (i + 1))
        source = source + mine * jnp.where(odd == 1, odd_k, even_k) * (lax.shift_right_logical(block, i) & 1)
    here = source == lax.broadcasted_iota(i32, (tokens, tokens), 1)

    def column(ref):
        return jnp.sum(jnp.where(here, ref[...], jnp.zeros_like(ref[...])), axis=1, keepdims=True)

    vocab = rank * cols + lax.broadcasted_iota(i32, (1, cols), 1)
    pick = (column(target) == vocab).astype(f32)
    took_o[...] = (column(ids) == vocab).astype(f32).astype(bf16)
    langs, blocks = allowed.shape
    speaks = (column(language) == lax.broadcasted_iota(i32, (1, langs), 1)).astype(f32)
    may = jnp.dot(speaks, allowed[...].astype(f32), preferred_element_type=f32)
    column_here = lax.broadcasted_iota(i32, (1, blocks), 1) == rank
    ok = jnp.sum(jnp.where(column_here, may, 0.0), axis=1, keepdims=True)
    code_o[...] = (jnp.where(ok > 0.0, 1.0, 0.0) * (1.0 + pick)).astype(bf16)
    weight_o[...] = jnp.broadcast_to(column(weight), weight_o.shape)
    upper = (rank & 1) == 1
    pick_o[...] = jnp.where(upper, jnp.concatenate([pick[half:], pick[:half]], 0), pick).astype(bf16)


def table_grad(tiles, dl, took, hid, inp, out, held, sem):
    lhs = jnp.concatenate([dl[...], took[...]], 0).T
    step = out.shape[1] // tiles
    leaving = []
    for i in range(tiles):
        at = pl.ds(i * step, step)
        rhs = jnp.concatenate([hid[:, at], inp[:, at]], 0)
        held[:, at] = jnp.dot(lhs, rhs, preferred_element_type=f32).astype(bf16)
        leaving.append(pltpu.make_async_copy(held.at[:, at], out.at[:, at], sem.at[i]))
        leaving[-1].start()
    for copy in leaving:
        copy.wait()


def per_device(n, hidden, embedding, d_input, input_ids, language, allowed, target, token_weight):
    cols, width = embedding.shape
    mine = hidden.shape[0]
    tokens = mine * n
    steps = n.bit_length() - 1
    me = lax.axis_index("vocab")

    def swap(x, k):
        ks = partners(n, k)
        return lax.ppermute(x, "vocab", [(i, i ^ ks[i & 1]) for i in range(n)])

    def bit(k):
        even_k, odd_k = partners(n, k)
        return (me & jnp.where((me & 1) == 1, odd_k, even_k)) != 0

    def after(x, *deps):
        return lax.optimization_barrier((x,) + deps)[0]

    def join(x, r, k):
        return jnp.where(bit(k), jnp.concatenate([r, x], 0), jnp.concatenate([x, r], 0))

    def halves(x, k):
        h = x.shape[0] // 2
        a, b = x[:h], x[h:]
        return jnp.where(bit(k), b, a), jnp.where(bit(k), a, b)

    first = swap(hidden, n // 2)
    first_input = swap(d_input, n // 2)
    vmem, hbm = pl.BlockSpec(memory_space=pltpu.VMEM), pl.BlockSpec(memory_space=pltpu.HBM)
    code, took, weight, pick = pl.pallas_call(
        functools.partial(prepare, mine, steps),
        out_shape=(
            jax.ShapeDtypeStruct((tokens, cols), bf16),
            jax.ShapeDtypeStruct((tokens, cols), bf16),
            jax.ShapeDtypeStruct((tokens, cols), f32),
            jax.ShapeDtypeStruct((tokens, cols), bf16),
        ),
        in_specs=[pl.BlockSpec(memory_space=pltpu.SMEM)] + [hbm] * 6,
        out_specs=(vmem,) * 4,
        scratch_shapes=[
            pltpu.VMEM((1, tokens), i32),
            pltpu.VMEM((1, tokens), i32),
            pltpu.VMEM(allowed.shape, i32),
            pltpu.VMEM((1, tokens), i32),
            pltpu.VMEM((1, tokens), f32),
            pltpu.SemaphoreType.DMA((5,)),
        ],
        compiler_params=pltpu.CompilerParams(vmem_limit_bytes=60 * 1024 * 1024),
        name="prepare",
    )(
        me.reshape(1, 1), embedding, input_ids.reshape(1, tokens), language.reshape(1, tokens),
        allowed, target.reshape(1, tokens), token_weight.reshape(1, tokens),
    )
    usable = code > 0
    is_target = code > 1

    k = n // 2
    all_hidden, all_input = join(hidden, first, k), join(d_input, first_input, k)
    k //= 2
    while k > 2:
        got, got_input = swap(all_hidden, k), swap(all_input, k)
        all_hidden, all_input = join(all_hidden, got, k), join(all_input, got_input, k)
        k //= 2
    got = swap(all_hidden, 2)
    half = tokens // 2
    rows = jnp.dot(after(pick, all_hidden), embedding, preferred_element_type=f32).astype(bf16)
    rows = rows[:half] + swap(rows[half:], 1)
    rows_keep, rows_send = halves(rows, 2)
    rows_got = swap(rows_send, 2)
    all_hidden = join(all_hidden, got, 2)
    input_got = swap(after(all_input, all_hidden), 2)
    all_hidden = join(all_hidden, swap(all_hidden, 1), 1)

    logits = lax.dot_general(all_hidden, embedding, (((1,), (1,)), ((), ())), preferred_element_type=f32)
    masked = jnp.where(usable, logits, f32(NEG))
    m = jnp.max(masked, axis=1)
    p = jnp.where(usable, jnp.exp(masked - m[:, None]), f32(0.0))
    s = jnp.sum(p, axis=1)
    lt = jnp.max(jnp.where(is_target, masked, f32(NEG)), axis=1)
    p = after(jnp.where(is_target, f32(0.0), p).astype(bf16), m, s, lt)
    part = jnp.dot(p, embedding, preferred_element_type=f32)

    lo = 0
    k = 1
    while k < n:
        last = k == n // 2
        keep, send = halves(part, k)
        send = send.astype(bf16)
        if last:
            rows_keep, rows_send = halves(rows, k)
            send = jnp.concatenate([send, rows_send], 0)
        packed = jnp.stack([m, s, lt])
        if k > 1:
            packed, send = lax.optimization_barrier((packed, send))
        got = swap(packed, k)
        recv = swap(send, k)
        size = keep.shape[0]
        if last:
            rows = rows_keep + recv[size:]
        m_new = jnp.maximum(m, got[0])
        a, b = jnp.exp(m - m_new), jnp.exp(got[0] - m_new)
        s = s * a + got[1] * b
        lt = jnp.maximum(lt, got[2])
        m, s, lt, a, b = lax.optimization_barrier((m_new, s, lt, a, b))
        if k == 1:
            all_input = join(all_input, after(input_got, m), 2)
            all_input = join(all_input, swap(all_input, 1), 1)
        lo = lo + jnp.where(bit(k), size, 0)
        part = keep * lax.dynamic_slice_in_dim(a, lo, size)[:, None] + recv[:size].astype(f32) * lax.dynamic_slice_in_dim(b, lo, size)[:, None]
        if k < n // 4:
            rows = rows_keep + after(rows_got, part)
        if k < n // 8:
            rows_keep, rows_send = halves(rows, 4 * k)
            rows_got = swap(rows_send, 4 * k)
        k *= 2

    hot = is_target.astype(f32)
    d_logits = jnp.where(
        usable, weight * (jnp.exp(masked - m[:, None]) / s[:, None] - hot), f32(0.0)
    ).astype(bf16)
    w = lax.dynamic_slice_in_dim(token_weight, me * mine, mine)
    m_own, s_own, lt_own = (lax.dynamic_slice_in_dim(x, lo, mine) for x in (m, s, lt))
    coef = (w * (jnp.exp(lt_own - m_own) / s_own - 1.0)).astype(bf16).astype(f32)
    d_hidden = (part * (w / s_own)[:, None] + rows.astype(f32) * coef[:, None]).astype(bf16)
    tiles = 8
    d_embed = pl.pallas_call(
        functools.partial(table_grad, tiles),
        out_shape=jax.ShapeDtypeStruct((cols, width), bf16),
        in_specs=[vmem] * 4,
        out_specs=hbm,
        scratch_shapes=[pltpu.VMEM((cols, width), bf16), pltpu.SemaphoreType.DMA((tiles,))],
        compiler_params=pltpu.CompilerParams(vmem_limit_bytes=24 * 1024 * 1024),
        cost_estimate=pl.CostEstimate(
            flops=4 * tokens * cols * width, bytes_accessed=2 * cols * width, transcendentals=0),
        name="table_grad",
    )(d_logits, took, all_hidden, all_input)
    return d_hidden, d_embed


def solution(mesh):
    n = mesh.shape["vocab"]
    placed = (
        P(("groups", "vocab"), None),
        P(("groups", "vocab"), None),
        P(("groups", "vocab"), None),
        P("groups"),
        P("groups"),
        P("groups", None),
        P("groups"),
        P("groups"),
    )
    return jax.shard_map(
        functools.partial(per_device, n),
        mesh=mesh,
        in_specs=placed,
        out_specs=(P(("groups", "vocab"), None), P(("groups", "vocab"), None)),
        check_vma=False,
    )
```
